128 devices in a mesh: layer: 8 (over z, x_hi), ex: 16 (over y, x_lo, core).
Axes of the slice: x: 4 (x_hi: 2, x_lo: 2; x = x_hi * 2 + x_lo), y: 4, z: 4, core: 2. Of those that a mesh axis runs over, the one named last changes fastest.
Arguments:
- train_grads: bfloat16 [8, 32768, 2048], P('layer', 'ex'), may hold values from -0.125 to 0.125
- query_grads: bfloat16 [8, 2048, 2048], P('layer', 'ex'), may hold values from -6 to 6
- inverses: bfloat16 [8, 2048, 2048], P('layer'), may hold values from -1 to 3
Outputs:
- kernel: float32 [32768, 2048], P('ex', 'layer')
The draws below stay inside these ranges and needn't reach their ends.
All inputs are finite; a program needn't handle non-finite values.
Results may differ from the reference program's by a relative error of at most 0.014.
Values may be sent and summed in bfloat16 or wider, within the bound.
No kernel may reach another device: no remote copies, remote signals or barrier semaphores. Data moves between devices by JAX's collectives and lax.ppermute only.
A program may use at most 128 MiB of HBM per device.

```python
import jax
import jax.numpy as jnp
from jax import lax

W = 2048
LAYERS = 8
NTR = 32768
NQ = 2048


def draw_inverses(key, part):
    key = jax.random.fold_in(key, 11)
    first, second = jax.random.split(key)
    spread = jax.random.normal(first, (LAYERS, W, W), jnp.float32)
    spread = jnp.clip(spread, -4.0, 4.0) * (0.5 / W ** 0.5)
    scales = jax.random.uniform(second, (LAYERS, W, 1), jnp.float32, 0.5, 2.0)
    rows = jax.lax.broadcasted_iota(jnp.int32, (1, W, W), 1)
    columns = jax.lax.broadcasted_iota(jnp.int32, (1, W, W), 2)
    matrix = jnp.where(rows == columns, scales, spread)
    return matrix.astype(jnp.bfloat16)


def levels(key, dims, cuts, smallest, largest):
    loudness = 1.0
    for position, parts in cuts:
        draws = jax.random.uniform(jax.random.fold_in(jax.random.fold_in(key, 6), position), (parts,), jnp.float32, smallest / len(cuts), largest / len(cuts))
        loudness = loudness * jnp.repeat(jnp.exp(draws), dims[position] // parts).reshape((-1,) + (1,) * (len(dims) - 1 - position))
    return loudness


def noise(stream_key, extent, width, bound, cuts=(), dtype=jnp.bfloat16):
    level = levels(stream_key, extent, cuts, -0.22, 0.18) if cuts else 1.0
    entries = jax.random.normal(stream_key, extent, jnp.float32) * width * level
    return jnp.minimum(jnp.maximum(entries, -bound), bound).astype(dtype)


def setup_inputs(seed: int = 0) -> dict:
    key_list = jax.random.split(jax.random.key(seed), 4)
    return {
        "train_grads": noise(key_list[0], (LAYERS, NTR, W), W ** -0.5, 0.125, ((0, 8), (1, 16))),
        "query_grads": noise(key_list[1], (LAYERS, NQ, W), 1.0, 6.0, ((0, 8), (1, 16))),
        "inverses": draw_inverses(jax.random.fold_in(key_list[3], 71), 0),
    }


def reference(train_grads, query_grads, inverses):
    total = jnp.zeros((train_grads.shape[1], query_grads.shape[1]), jnp.float32)
    for layer_index in range(LAYERS):
        conditioned = jnp.dot(query_grads[layer_index], inverses[layer_index], preferred_element_type=jnp.float32).astype(jnp.bfloat16)
        layer_kernel = jnp.dot(train_grads[layer_index], conditioned.T, preferred_element_type=jnp.float32).astype(jnp.bfloat16)
        layer_kernel = lax.optimization_barrier(layer_kernel)
        total = total + layer_kernel.astype(jnp.float32)
    return total
```

```python
import jax
import jax.numpy as jnp
from jax import lax
from jax.sharding import PartitionSpec as P

Z, XH, Y, XL, CORE = 4, 2, 4, 2, 2
X_FIRST = 512


def device(z, h, y, x, c):
    return ((z % Z) * XH + h % XH) * (Y * XL * CORE) + ((y % Y) * XL + x % XL) * CORE + c % CORE


def route(dz=0, dh=0, dy=0, dx=0, dc=0, only=None):
    return [
        (device(z, h, y, x, c), device(z + dz, h + dh, y + dy, x + dx, c + dc))
        for z in range(Z)
        for h in range(XH)
        for y in range(Y)
        for x in range(XL)
        for c in range(CORE)
        if only is None or only(h, x)
    ]


def send(block, **where):
    return lax.ppermute(block, ("layer", "ex"), route(**where))


def product(rows, queries):
    return jnp.einsum("tw,qw->tq", rows, queries, preferred_element_type=jnp.float32)


def narrow(value):
    return value.astype(jnp.bfloat16)


def wide(value):
    return value.astype(jnp.float32)


def tree(parts):
    up2, down2 = parts(2)
    far_up = send(up2, dz=-1)
    far_down = send(down2, dz=1)
    up1, down1 = parts(1)
    up3, down3 = parts(3)
    near_up = send(up1, dz=1)
    near_down = send(down3, dz=-1)
    merged_up = send(narrow(wide(up3) + wide(far_up)), dz=-1)
    merged_down = send(narrow(wide(down1) + wide(far_down)), dz=1)
    up0, down0 = parts(0)
    up = wide(up0) + wide(near_up) + wide(merged_up)
    down = wide(down0) + wide(near_down) + wide(merged_down)
    return jnp.concatenate([up, down], 0)


def on_device(train_grads, query_grads, inverses):
    layer, ex = lax.axis_index("layer"), lax.axis_index("ex")
    z, h = layer >> 1, layer & 1
    y, x, core = ex >> 2, (ex >> 1) & 1, ex & 1
    train, query, inverse = train_grads[0], query_grads[0], inverses[0]
    rows = train.shape[0]
    first = rows - X_FIRST
    cuts = [(0, first // 2), (first // 2, first), (first, rows)]

    near = {0: query}
    near[3] = send(query, dy=1)
    near[1] = send(query, dy=-1)
    near[2] = send(query, dy=2)
    far = {0: send(query, dx=1)}
    far[3] = send(far[0], dy=1)
    far[1] = send(far[0], dy=-1)
    far[2] = send(near[2], dx=1)

    mixed = [
        narrow(jnp.einsum("tv,wv->tw", train[a:b], inverse, preferred_element_type=jnp.float32)) for a, b in cuts
    ]

    def columns(found):
        mine = jnp.stack([found[k] for k in range(Y)])
        other = send(mine, dc=1)
        return jnp.stack([mine, other], 1).reshape(Y, CORE * query.shape[0], query.shape[1])

    def z_first(queries):
        def parts(j):
            chosen = lax.dynamic_index_in_dim(queries, (z + j - y) & (Y - 1), 0, keepdims=False)
            return narrow(product(mixed[0], chosen)), narrow(product(mixed[1], chosen))

        return tree(parts)

    same = h == x
    queries = [columns(near), columns(far)]
    flat = [q.reshape(-1, q.shape[-1]) for q in queries]
    crossing = [narrow(product(mixed[2], q)) for q in flat]
    sources = [lambda h, x: h != x, lambda h, x: h == x]
    sums = [z_first(q) for q in queries]
    came = [send(crossing[k], dh=1, only=sources[k]) for k in range(2)]
    paired = jnp.where(same, wide(crossing[0]) + wide(came[0]), wide(crossing[1]) + wide(came[1]))
    paired = narrow(paired).reshape(X_FIRST, Y, -1).transpose(1, 0, 2)

    def parts(j):
        chosen = lax.dynamic_index_in_dim(paired, (z + j - y) & (Y - 1), 0, keepdims=False)
        return chosen[: X_FIRST // 2], chosen[X_FIRST // 2 :]

    arrived = [send(narrow(sums[k]), dh=1, only=sources[k]) for k in range(2)]
    upper = jnp.where(same, sums[0] + wide(arrived[0]), sums[1] + wide(arrived[1]))
    lower = tree(parts)
    kernel = jnp.concatenate([upper, lower], 0)
    half = kernel.shape[1] // 2
    return jnp.where(core == 0, kernel, jnp.concatenate([kernel[:, half:], kernel[:, :half]], 1))


def solution(mesh):
    return jax.shard_map(
        on_device,
        mesh=mesh,
        in_specs=(P("layer", "ex", None), P("layer", "ex", None), P("layer", None, None)),
        out_specs=P("ex", "layer"),
        check_vma=False,
    )
```

```python
import jax
import jax.numpy as jnp
from jax import lax
from jax.sharding import PartitionSpec as P

Z, XH, Y, XL, CORE = 4, 2, 4, 2, 2
X_FIRST = 512


def device(z, h, y, x, c):
    return ((z % Z) * XH + h % XH) * (Y * XL * CORE) + ((y % Y) * XL + x % XL) * CORE + c % CORE


def route(dz=0, dh=0, dy=0, dx=0, dc=0, only=None):
    return [
        (device(z, h, y, x, c), device(z + dz, h + dh, y + dy, x + dx, c + dc))
        for z in range(Z)
        for h in range(XH)
        for y in range(Y)
        for x in range(XL)
        for c in range(CORE)
        if only is None or only(h, x)
    ]


def send(block, **where):
    return lax.ppermute(block, ("layer", "ex"), route(**where))


def narrow(value):
    return value.astype(jnp.bfloat16)


def wide(value):
    return value.astype(jnp.float32)


def product(rows, queries):
    return narrow(jnp.einsum("tw,qw->tq", rows, queries, preferred_element_type=jnp.float32))


def after(value, *earlier):
    return lax.optimization_barrier((value, earlier))[0]


def both_ways(back, ahead):
    return send(back, dz=-1), send(ahead, dz=1)


def merge(mine, came):
    return [narrow(wide(m) + wide(c)) for m, c in zip(mine, came)]


def total(*terms):
    return jnp.concatenate([sum(wide(t) for t in side) for side in zip(*terms)], 0)


def on_device(train_grads, query_grads, inverses):
    layer, ex = lax.axis_index("layer"), lax.axis_index("ex")
    z, h = layer >> 1, layer & 1
    y, x, core = ex >> 2, (ex >> 1) & 1, ex & 1
    train, own = train_grads[0], query_grads[0]
    rows, count = train.shape[0], own.shape[0]
    first = rows - X_FIRST
    same = h == x

    own = narrow(jnp.dot(own, inverses[0], preferred_element_type=jnp.float32))
    upper, lower, crossing = train[: first // 2], train[first // 2 : first], train[first:]
    near3, near1, far0 = send(own, dy=1), send(own, dy=-1), send(own, dx=1)
    own_other = send(own, dc=1)
    near1, near3 = after((near1, near3), far0)
    half = count // 2
    near2 = jnp.concatenate([send(near3[:half], dy=1), send(near1[half:], dy=-1)], 0)
    beside_other = send(near1, dc=1), send(near3, dc=1)
    near2_other = send(near2, dc=1)
    far1, far3, far2 = send(far0, dy=-1), send(far0, dy=1), send(near2, dx=1)

    def pick(mine, other, j):
        k = (z + j - y) & (Y - 1)

        def at(found):
            return jnp.where(k < 2, jnp.where(k == 0, found[0], found[1]), jnp.where(k == 2, found[2], found[3]))

        m, o = at(mine), at(other)
        return jnp.where(core == 0, jnp.concatenate([m, o], 0), jnp.concatenate([o, m], 0))

    def halves(q_up, q_down):
        return product(upper, q_up), product(lower, q_down)

    def crossed(q):
        return jnp.concatenate([product(crossing, q[j]) for j in range(Z)], 1)

    def lead(q):
        far, near = halves(q[2], q[2]), halves(q[1], q[3])
        return jnp.concatenate([far[0], near[1]], 0), jnp.concatenate([far[1], near[0]], 0)

    def parted(back, ahead):
        n = back.shape[0] // 2
        return (back[:n], ahead[:n]), (ahead[n:], back[n:])

    near_mine = [own, near1, near2, near3]
    near_other = [own_other, beside_other[0], near2_other, beside_other[1]]
    qa = [pick(near_mine, near_other, j) for j in range(Z)]
    lead_a = lead(qa)
    came_a, near_a = parted(*both_ways(*lead_a))
    far_mine, qa = after(([far0, far1, far2, far3], qa), lead_a)
    far_other = send(jnp.stack(far_mine), dc=1)
    xa = crossed(qa)
    qa = after(qa, xa)
    mine_a, own_a = halves(qa[3], qa[1]), halves(qa[0], qa[0])

    qb = after([pick(far_mine, far_other, j) for j in range(Z)], mine_a, own_a)
    xb = crossed(qb)
    cross = send(jnp.where(same, xb, xa), dh=1)
    qb = after(qb, xb)
    lead_b = lead(qb)
    back, ahead = both_ways(*lead_b)
    came_b, near_b = parted(back, ahead)
    qb = after(qb, lead_b)
    last_a = merge(mine_a, after(came_a, lead_b))
    last_a_in = both_ways(*last_a)
    mine_b = halves(qb[3], qb[1])
    last_b = merge(mine_b, after(came_b, last_a, mine_b))
    last_b_in = both_ways(*last_b)
    qb = after(qb, last_b)
    own_b = halves(qb[0], qb[0])

    paired = narrow(wide(jnp.where(same, xa, xb)) + wide(after(cross, last_b)))
    width = paired.shape[1] // Z
    blocks = [paired[:, j * width : (j + 1) * width] for j in range(Z)]
    direct = [send(blocks[j], dz=j) for j in (1, 2, 3)]

    sum_a = total(own_a, near_a, last_a_in)
    sum_b = total(own_b, near_b, last_b_in)
    arrived = send(narrow(jnp.where(same, sum_b, sum_a)), dh=1)
    sum_r = wide(blocks[0]) + sum(wide(d) for d in direct)
    top = jnp.where(same, sum_a, sum_b) + wide(arrived)
    return jnp.concatenate([top, sum_r], 0)


def solution(mesh):
    return jax.shard_map(
        on_device,
        mesh=mesh,
        in_specs=(P("layer", "ex", None), P("layer", "ex", None), P("layer", None, None)),
        out_specs=P("ex", "layer"),
        check_vma=False,
    )
```

```python
import jax
import jax.numpy as jnp
from jax import lax
from jax.sharding import PartitionSpec as P

Z, XH, Y, XL, CORE = 4, 2, 4, 2, 2
X_FIRST = 512


def device(z, h, y, x, c):
    return ((z % Z) * XH + h % XH) * (Y * XL * CORE) + ((y % Y) * XL + x % XL) * CORE + c % CORE


def route(dz=0, dh=0, dy=0, dx=0, dc=0, only=None):
    return [
        (device(z, h, y, x, c), device(z + dz, h + dh, y + dy, x + dx, c + dc))
        for z in range(Z)
        for h in range(XH)
        for y in range(Y)
        for x in range(XL)
        for c in range(CORE)
        if only is None or only(h, x)
    ]


def send(block, **where):
    return lax.ppermute(block, ("layer", "ex"), route(**where))


def narrow(value):
    return value.astype(jnp.bfloat16)


def wide(value):
    return value.astype(jnp.float32)


def product(rows, queries):
    return narrow(jnp.einsum("tw,qw->tq", rows, queries, preferred_element_type=jnp.float32))


def after(value, *earlier):
    return lax.optimization_barrier((value, earlier))[0]


def both_ways(back, ahead):
    return send(back, dz=-1), send(ahead, dz=1)


def merge(mine, came):
    return [narrow(wide(m) + wide(c)) for m, c in zip(mine, came)]


def total(*terms):
    return jnp.concatenate([sum(wide(t) for t in side) for side in zip(*terms)], 0)


def on_device(train_grads, query_grads, inverses):
    layer, ex = lax.axis_index("layer"), lax.axis_index("ex")
    z, h = layer >> 1, layer & 1
    y, x, core = ex >> 2, (ex >> 1) & 1, ex & 1
    train, own = train_grads[0], query_grads[0]
    rows, count = train.shape[0], own.shape[0]
    first = rows - X_FIRST
    same = h == x

    own = narrow(jnp.dot(own, inverses[0], preferred_element_type=jnp.float32))
    upper, lower, crossing = train[: first // 2], train[first // 2 : first], train[first:]
    near3, near1, far0 = send(own, dy=1), send(own, dy=-1), send(own, dx=1)
    own_other = send(own, dc=1)
    near1, near3 = after((near1, near3), far0)
    half = count // 2
    near2 = jnp.concatenate([send(near3[:half], dy=1), send(near1[half:], dy=-1)], 0)
    beside_other = send(near1, dc=1), send(near3, dc=1)
    near2_other = send(near2, dc=1)
    far1, far3, far2 = send(far0, dy=-1), send(far0, dy=1), send(near2, dx=1)

    def pick(mine, other, j):
        k = (z + j - y) & (Y - 1)

        def at(found):
            return jnp.where(k < 2, jnp.where(k == 0, found[0], found[1]), jnp.where(k == 2, found[2], found[3]))

        m, o = at(mine), at(other)
        return jnp.where(core == 0, jnp.concatenate([m, o], 0), jnp.concatenate([o, m], 0))

    def halves(q_up, q_down):
        return product(upper, q_up), product(lower, q_down)

    def crossed(q):
        return jnp.concatenate([product(crossing, q[j]) for j in range(Z)], 1)

    def lead(q):
        far, near = halves(q[2], q[2]), halves(q[1], q[3])
        return jnp.concatenate([far[0], near[1]], 0), jnp.concatenate([far[1], near[0]], 0)

    def parted(back, ahead):
        n = back.shape[0] // 2
        return (back[:n], ahead[:n]), (ahead[n:], back[n:])

    near_mine = [own, near1, near2, near3]
    near_other = [own_other, beside_other[0], near2_other, beside_other[1]]
    qa = [pick(near_mine, near_other, j) for j in range(Z)]
    lead_a = lead(qa)
    back_a, ahead_a = both_ways(*lead_a)
    qa, far_mine = after((qa, [far0, far1, far2, far3]), lead_a)
    far_other = [*send(jnp.stack(far_mine[:2]), dc=1), *send(jnp.stack(far_mine[2:]), dc=1)]
    xa = crossed(qa)
    qa = after(qa, xa)
    own_a = halves(qa[0], qa[0])

    qb = after([pick(far_mine, far_other, j) for j in range(Z)], own_a)
    xb = crossed(qb)
    cross = send(jnp.where(same, xb, xa), dh=1)
    qb = after(qb, xb)
    lead_b = lead(qb)
    back_b, ahead_b = both_ways(*lead_b)

    back_a, ahead_a = after((back_a, ahead_a), lead_b)
    came_a, near_a = parted(back_a, ahead_a)
    qa = after(qa, back_a, ahead_a)
    last_a = merge(halves(qa[3], qa[1]), came_a)
    last_a_in = both_ways(*last_a)
    qb = after(qb, last_a)
    mine_b = halves(qb[3], qb[1])
    came_b, near_b = parted(*after((back_b, ahead_b), mine_b))
    last_b = merge(mine_b, came_b)
    last_b_in = both_ways(*last_b)
    qb = after(qb, last_b)
    own_b = halves(qb[0], qb[0])

    paired = narrow(wide(jnp.where(same, xa, xb)) + wide(after(cross, last_b)))
    width = paired.shape[1] // Z
    blocks = [paired[:, j * width : (j + 1) * width] for j in range(Z)]
    direct = [send(blocks[j], dz=j) for j in (1, 2, 3)]

    sum_a = total(own_a, near_a, last_a_in)
    sum_b = total(own_b, near_b, last_b_in)
    arrived = send(narrow(jnp.where(same, sum_b, sum_a)), dh=1)
    sum_r = wide(blocks[0]) + sum(wide(d) for d in direct)
    top = jnp.where(same, sum_a, sum_b) + wide(arrived)
    return jnp.concatenate([top, sum_r], 0)


def solution(mesh):
    return jax.shard_map(
        on_device,
        mesh=mesh,
        in_specs=(P("layer", "ex", None), P("layer", "ex", None), P("layer", None, None)),
        out_specs=P("ex", "layer"),
        check_vma=False,
    )
```

```python
import jax
import jax.numpy as jnp
from jax import lax
from jax.sharding import PartitionSpec as P

Z, XH, Y, XL, CORE = 4, 2, 4, 2, 2
X_FIRST = 640


def device(z, h, y, x, c):
    return ((z % Z) * XH + h % XH) * (Y * XL * CORE) + ((y % Y) * XL + x % XL) * CORE + c % CORE


def route(dz=0, dh=0, dy=0, dx=0, dc=0, only=None):
    return [
        (device(z, h, y, x, c), device(z + dz, h + dh, y + dy, x + dx, c + dc))
        for z in range(Z)
        for h in range(XH)
        for y in range(Y)
        for x in range(XL)
        for c in range(CORE)
        if only is None or only(h, x)
    ]


def send(block, **where):
    return lax.ppermute(block, ("layer", "ex"), route(**where))


def narrow(value):
    return value.astype(jnp.bfloat16)


def wide(value):
    return value.astype(jnp.float32)


def product(rows, queries):
    return narrow(jnp.einsum("tw,qw->tq", rows, queries, preferred_element_type=jnp.float32))


def after(value, *earlier):
    return lax.optimization_barrier((value, earlier))[0]


def both_ways(back, ahead):
    return send(back, dz=-1), send(ahead, dz=1)


def merge(mine, came):
    return [narrow(wide(m) + wide(c)) for m, c in zip(mine, came)]


def total(*terms):
    return jnp.concatenate([sum(wide(t) for t in side) for side in zip(*terms)], 0)


def on_device(train_grads, query_grads, inverses):
    layer, ex = lax.axis_index("layer"), lax.axis_index("ex")
    z, h = layer >> 1, layer & 1
    y, x, core = ex >> 2, (ex >> 1) & 1, ex & 1
    train, own = train_grads[0], query_grads[0]
    rows, count = train.shape[0], own.shape[0]
    first = rows - X_FIRST
    same = h == x

    own = narrow(jnp.dot(own, inverses[0], preferred_element_type=jnp.float32))
    upper, lower, crossing = train[: first // 2], train[first // 2 : first], train[first:]
    near3, near1, far0 = send(own, dy=1), send(own, dy=-1), send(own, dx=1)
    own_other = send(own, dc=1)
    near1, near3 = after((near1, near3), far0)
    half = count // 2
    near2 = jnp.concatenate([send(near3[:half], dy=1), send(near1[half:], dy=-1)], 0)
    beside_other = send(near1, dc=1), send(near3, dc=1)
    near2_other = send(near2, dc=1)
    far1, far3, far2 = send(far0, dy=-1), send(far0, dy=1), send(near2, dx=1)

    def pick(mine, other, j):
        k = (z + j - y) & (Y - 1)

        def at(found):
            return jnp.where(k < 2, jnp.where(k == 0, found[0], found[1]), jnp.where(k == 2, found[2], found[3]))

        m, o = at(mine), at(other)
        return jnp.where(core == 0, jnp.concatenate([m, o], 0), jnp.concatenate([o, m], 0))

    def halves(q_up, q_down):
        return product(upper, q_up), product(lower, q_down)

    def crossed(q):
        return jnp.concatenate([product(crossing, q[j]) for j in range(Z)], 1)

    def lead(q):
        far, near = halves(q[2], q[2]), halves(q[1], q[3])
        return jnp.concatenate([far[0], near[1]], 0), jnp.concatenate([far[1], near[0]], 0)

    def parted(back, ahead):
        n = back.shape[0] // 2
        return (back[:n], ahead[:n]), (ahead[n:], back[n:])

    near_mine = [own, near1, near2, near3]
    near_other = [own_other, beside_other[0], near2_other, beside_other[1]]
    qa = [pick(near_mine, near_other, j) for j in range(Z)]
    lead_a = lead(qa)
    came_a, near_a = parted(*both_ways(*lead_a))
    qa = after(qa, lead_a)
    xa = crossed(qa)
    far_mine = after([far0, far1, far2, far3], xa)
    far_other = [send(block, dc=1) for block in far_mine]
    qa = after(qa, xa)
    mine_a, own_a = halves(qa[3], qa[1]), halves(qa[0], qa[0])

    qb = after([pick(far_mine, far_other, j) for j in range(Z)], mine_a, own_a)
    xb = crossed(qb)
    cross = send(jnp.where(same, xb, xa), dh=1)
    qb = after(qb, xb)
    lead_b = lead(qb)
    back, ahead = both_ways(*lead_b)
    came_b, near_b = parted(back, ahead)
    qb = after(qb, lead_b)
    last_a = merge(mine_a, after(came_a, lead_b))
    last_a_in = both_ways(*last_a)
    mine_b = halves(qb[3], qb[1])
    last_b = merge(mine_b, after(came_b, last_a, mine_b, cross))
    last_b_in = both_ways(*last_b)
    qb = after(qb, last_b)
    own_b = halves(qb[0], qb[0])

    paired = narrow(wide(jnp.where(same, xa, xb)) + wide(after(cross, last_b)))
    width = paired.shape[1] // Z
    blocks = [paired[:, j * width : (j + 1) * width] for j in range(Z)]
    direct = [send(blocks[j], dz=j) for j in (1, 2, 3)]

    sum_a = total(own_a, near_a, last_a_in)
    sum_b = total(own_b, near_b, last_b_in)
    arrived = send(narrow(jnp.where(same, sum_b, sum_a)), dh=1)
    sum_r = wide(blocks[0]) + sum(wide(d) for d in direct)
    top = jnp.where(same, sum_a, sum_b) + wide(arrived)
    return jnp.concatenate([top, sum_r], 0)


def solution(mesh):
    return jax.shard_map(
        on_device,
        mesh=mesh,
        in_specs=(P("layer", "ex", None), P("layer", "ex", None), P("layer", None, None)),
        out_specs=P("ex", "layer"),
        check_vma=False,
    )
```

```python
import jax
import jax.numpy as jnp
from jax import lax
from jax.sharding import PartitionSpec as P

Z, XH, Y, XL, CORE = 4, 2, 4, 2, 2
X_FIRST = 640


def device(z, h, y, x, c):
    return ((z % Z) * XH + h % XH) * (Y * XL * CORE) + ((y % Y) * XL + x % XL) * CORE + c % CORE


def route(dz=0, dh=0, dy=0, dx=0, dc=0, only=None):
    return [
        (device(z, h, y, x, c), device(z + dz, h + dh, y + dy, x + dx, c + dc))
        for z in range(Z)
        for h in range(XH)
        for y in range(Y)
        for x in range(XL)
        for c in range(CORE)
        if only is None or only(h, x)
    ]


def send(block, **where):
    return lax.ppermute(block, ("layer", "ex"), route(**where))


def narrow(value):
    return value.astype(jnp.bfloat16)


def wide(value):
    return value.astype(jnp.float32)


def product(rows, queries):
    return narrow(jnp.einsum("tw,qw->tq", rows, queries, preferred_element_type=jnp.float32))


def after(value, *earlier):
    return lax.optimization_barrier((value, earlier))[0]


def both_ways(back, ahead):
    return send(back, dz=-1), send(ahead, dz=1)


def merge(mine, came):
    return [narrow(wide(m) + wide(c)) for m, c in zip(mine, came)]


def total(*terms):
    return jnp.concatenate([sum(wide(t) for t in side) for side in zip(*terms)], 0)


def on_device(train_grads, query_grads, inverses):
    layer, ex = lax.axis_index("layer"), lax.axis_index("ex")
    z, h = layer >> 1, layer & 1
    y, x, core = ex >> 2, (ex >> 1) & 1, ex & 1
    train, own = train_grads[0], query_grads[0]
    rows, count = train.shape[0], own.shape[0]
    first = rows - X_FIRST
    same = h == x

    own = narrow(jnp.dot(own, inverses[0], preferred_element_type=jnp.float32))
    upper, lower, crossing = train[: first // 2], train[first // 2 : first], train[first:]
    near3, near1, far0 = send(own, dy=1), send(own, dy=-1), send(own, dx=1)
    own_other = send(own, dc=1)
    half = count // 2
    near2 = jnp.concatenate([send(near3[:half], dy=1), send(near1[half:], dy=-1)], 0)
    beside_other = send(near1, dc=1), send(near3, dc=1)
    near2_other = send(near2, dc=1)
    far1, far3, far2 = send(far0, dy=-1), send(far0, dy=1), send(near2, dx=1)

    def pick(mine, other, j):
        k = (z + j - y) & (Y - 1)

        def at(found):
            return jnp.where(k < 2, jnp.where(k == 0, found[0], found[1]), jnp.where(k == 2, found[2], found[3]))

        m, o = at(mine), at(other)
        return jnp.where(core == 0, jnp.concatenate([m, o], 0), jnp.concatenate([o, m], 0))

    def halves(q_up, q_down):
        return product(upper, q_up), product(lower, q_down)

    def crossed(q):
        return jnp.concatenate([product(crossing, q[j]) for j in range(Z)], 1)

    def lead(q):
        far, near = halves(q[2], q[2]), halves(q[1], q[3])
        return jnp.concatenate([far[0], near[1]], 0), jnp.concatenate([far[1], near[0]], 0)

    def parted(back, ahead):
        n = back.shape[0] // 2
        return (back[:n], ahead[:n]), (ahead[n:], back[n:])

    near_mine = [own, near1, near2, near3]
    near_other = [own_other, beside_other[0], near2_other, beside_other[1]]
    qa = [pick(near_mine, near_other, j) for j in range(Z)]
    lead_a = lead(qa)
    came_a, near_a = parted(*both_ways(*lead_a))
    qa = after(qa, lead_a)
    xa = crossed(qa)
    far_mine = after([far0, far1, far2, far3], xa)
    far_other = [send(block, dc=1) for block in far_mine]
    qa = after(qa, xa)
    mine_a, own_a = halves(qa[3], qa[1]), halves(qa[0], qa[0])

    qb = after([pick(far_mine, far_other, j) for j in range(Z)], mine_a, own_a)
    xb = crossed(qb)
    cross = send(jnp.where(same, xb, xa), dh=1)
    qb = after(qb, xb)
    lead_b = lead(qb)
    back, ahead = both_ways(*lead_b)
    came_b, near_b = parted(back, ahead)
    qb = after(qb, lead_b)
    last_a = merge(mine_a, after(came_a, lead_b))
    last_a_in = both_ways(*last_a)
    mine_b = halves(qb[3], qb[1])
    last_b = merge(mine_b, after(came_b, last_a, mine_b, cross))
    last_b_in = both_ways(*last_b)
    qb = after(qb, last_b)
    own_b = halves(qb[0], qb[0])

    paired = narrow(wide(jnp.where(same, xa, xb)) + wide(after(cross, last_b)))
    width = paired.shape[1] // Z
    blocks = [paired[:, j * width : (j + 1) * width] for j in range(Z)]
    direct = [send(blocks[j], dz=j) for j in (1, 2, 3)]

    sum_a = total(own_a, near_a, last_a_in)
    sum_b = total(own_b, near_b, last_b_in)
    arrived = send(narrow(jnp.where(same, sum_b, sum_a)), dh=1)
    sum_r = wide(blocks[0]) + sum(wide(d) for d in direct)
    top = jnp.where(same, sum_a, sum_b) + wide(arrived)
    return jnp.concatenate([top, sum_r], 0)


def solution(mesh):
    return jax.shard_map(
        on_device,
        mesh=mesh,
        in_specs=(P("layer", "ex", None), P("layer", "ex", None), P("layer", None, None)),
        out_specs=P("ex", "layer"),
        check_vma=False,
    )
```

```python
import jax
import jax.numpy as jnp
from jax import lax
from jax.sharding import PartitionSpec as P

Z, XH, Y, XL, CORE = 4, 2, 4, 2, 2
X_FIRST = 608


def device(z, h, y, x, c):
    return ((z % Z) * XH + h % XH) * (Y * XL * CORE) + ((y % Y) * XL + x % XL) * CORE + c % CORE


def route(dz=0, dh=0, dy=0, dx=0, dc=0, only=None):
    return [
        (device(z, h, y, x, c), device(z + dz, h + dh, y + dy, x + dx, c + dc))
        for z in range(Z)
        for h in range(XH)
        for y in range(Y)
        for x in range(XL)
        for c in range(CORE)
        if only is None or only(h, x)
    ]


def send(block, **where):
    return lax.ppermute(block, ("layer", "ex"), route(**where))


def narrow(value):
    return value.astype(jnp.bfloat16)


def wide(value):
    return value.astype(jnp.float32)


def product(rows, queries):
    return narrow(jnp.einsum("tw,qw->tq", rows, queries, preferred_element_type=jnp.float32))


def after(value, *earlier):
    return lax.optimization_barrier((value, earlier))[0]


def both_ways(back, ahead):
    return send(back, dz=-1), send(ahead, dz=1)


def merge(mine, came):
    return [narrow(wide(m) + wide(c)) for m, c in zip(mine, came)]


def total(*terms):
    return jnp.concatenate([sum(wide(t) for t in side) for side in zip(*terms)], 0)


def on_device(train_grads, query_grads, inverses):
    layer, ex = lax.axis_index("layer"), lax.axis_index("ex")
    z, h = layer >> 1, layer & 1
    y, x, core = ex >> 2, (ex >> 1) & 1, ex & 1
    train, own = train_grads[0], query_grads[0]
    rows, count = train.shape[0], own.shape[0]
    first = rows - X_FIRST
    same = h == x

    own = narrow(jnp.dot(own, inverses[0], preferred_element_type=jnp.float32))
    upper, lower, crossing = train[: first // 2], train[first // 2 : first], train[first:]
    near3, near1, far0 = send(own, dy=1), send(own, dy=-1), send(own, dx=1)
    own_other = send(own, dc=1)
    near1, near3 = after((near1, near3), far0)
    half = count // 2
    near2 = jnp.concatenate([send(near3[:half], dy=1), send(near1[half:], dy=-1)], 0)
    beside_other = send(near1, dc=1), send(near3, dc=1)
    near2_other = send(near2, dc=1)
    far1, far3, far2 = send(far0, dy=-1), send(far0, dy=1), send(near2, dx=1)

    def pick(mine, other, j):
        k = (z + j - y) & (Y - 1)

        def at(found):
            return jnp.where(k < 2, jnp.where(k == 0, found[0], found[1]), jnp.where(k == 2, found[2], found[3]))

        m, o = at(mine), at(other)
        return jnp.where(core == 0, jnp.concatenate([m, o], 0), jnp.concatenate([o, m], 0))

    def halves(q_up, q_down):
        return product(upper, q_up), product(lower, q_down)

    def crossed(q):
        return jnp.concatenate([product(crossing, q[j]) for j in range(Z)], 1)

    def lead(q):
        far, near = halves(q[2], q[2]), halves(q[1], q[3])
        return jnp.concatenate([far[0], near[1]], 0), jnp.concatenate([far[1], near[0]], 0)

    def parted(back, ahead):
        n = back.shape[0] // 2
        return (back[:n], ahead[:n]), (ahead[n:], back[n:])

    near_mine = [own, near1, near2, near3]
    near_other = [own_other, beside_other[0], near2_other, beside_other[1]]
    qa = [pick(near_mine, near_other, j) for j in range(Z)]
    lead_a = lead(qa)
    came_a, near_a = parted(*both_ways(*lead_a))
    qa = after(qa, lead_a)
    xa = crossed(qa)
    far_mine = after([far0, far1, far2, far3], xa)
    far_other = [send(block, dc=1) for block in far_mine]
    qa = after(qa, xa)
    mine_a, own_a = halves(qa[3], qa[1]), halves(qa[0], qa[0])

    qb = after([pick(far_mine, far_other, j) for j in range(Z)], mine_a, own_a)
    xb = crossed(qb)
    cross = send(jnp.where(same, xb, xa), dh=1)
    qb = after(qb, xb)
    lead_b = lead(qb)
    back, ahead = both_ways(*lead_b)
    came_b, near_b = parted(back, ahead)
    qb = after(qb, lead_b)
    last_a = merge(mine_a, after(came_a, lead_b))
    last_a_in = both_ways(*last_a)
    mine_b = halves(qb[3], qb[1])
    last_b = merge(mine_b, after(came_b, last_a, mine_b, cross))
    last_b_in = both_ways(*last_b)
    qb = after(qb, last_b)
    own_b = halves(qb[0], qb[0])

    paired = narrow(wide(jnp.where(same, xa, xb)) + wide(after(cross, last_b)))
    width = paired.shape[1] // Z
    blocks = [paired[:, j * width : (j + 1) * width] for j in range(Z)]
    direct = [send(blocks[j], dz=j) for j in (1, 2, 3)]

    sum_a = total(own_a, near_a, last_a_in)
    sum_b = total(own_b, near_b, last_b_in)
    arrived = send(narrow(jnp.where(same, sum_b, sum_a)), dh=1)
    sum_r = wide(blocks[0]) + sum(wide(d) for d in direct)
    top = jnp.where(same, sum_a, sum_b) + wide(arrived)
    return jnp.concatenate([top, sum_r], 0)


def solution(mesh):
    return jax.shard_map(
        on_device,
        mesh=mesh,
        in_specs=(P("layer", "ex", None), P("layer", "ex", None), P("layer", None, None)),
        out_specs=P("ex", "layer"),
        check_vma=False,
    )
```
